32 devices in a mesh: blk: 4 (over y, x), head: 8 (over z, core).
Axes of the slice: x: 2, y: 2, z: 4, core: 2. Of those that a mesh axis runs over, the one named last changes fastest.
Arguments:
- queries: bfloat16 [4096, 4096], P(('blk', 'head')), may hold values from -14 to 14
- keys: bfloat16 [4096, 4096], P(('blk', 'head')), may hold values from -14 to 14
- values: bfloat16 [4096, 4096], P(('blk', 'head')), may hold values from -15 to 15
- key_blocks: int32 [8, 6], replicated, may hold values from 0 to 7, as said below
- counts: int32 [8], replicated, may hold values from 3 to 6, as said below
Outputs:
- attended: bfloat16 [4096, 4096], P(('blk', 'head'))
The draws below stay inside these ranges and needn't reach their ends.
Inputs may be any that keep to these rules, and one draw needn't show every extreme that they name: `key_blocks`: row b lists, in slots below counts[b], distinct key blocks that lie in the cycle shard of b (shard = block // 2) or in one of the two shards beside it on the closed cycle of 4 shards; slots 0, 1, 2 hold b, b - 1 and b + 1 modulo 8; unused slots repeat slot 0. `counts`: some row uses all 6 slots and some row uses 3.
All inputs are finite; a program needn't handle non-finite values.
Results may differ from the reference program's by a relative error of at most 0.0036.
Values may be sent and summed in bfloat16 or wider, within the bound.
A program may use at most 64 MiB of HBM per device.

```python
import jax
import jax.numpy as jnp
from jax import lax

HEADS = 32
HD = 128
D = 4096
BLOCK = 512
MAXB = 6
SHARD_BLOCKS = 2
QBLOCKS = 8
TOKENS = 4096


def draw_queries(key, part):
    base = 2.0 * jnp.clip(jax.random.normal(jax.random.fold_in(key, 1), (TOKENS, D), jnp.float32), -4.0, 4.0)
    return base.astype(jnp.bfloat16)


def draw_keys(key, part):
    base = jnp.clip(jax.random.normal(jax.random.fold_in(key, 2), (TOKENS, D), jnp.float32), -5.0, 5.0)
    return base.astype(jnp.bfloat16)


def block_pattern(key):
    span = 3 * SHARD_BLOCKS
    rows = jnp.arange(QBLOCKS, dtype=jnp.int32)
    local = rows % SHARD_BLOCKS
    shard = rows // SHARD_BLOCKS
    offsets = jnp.arange(span, dtype=jnp.int32)
    row_keys = jax.random.split(jax.random.fold_in(key, 7), QBLOCKS)
    shuffled = jax.vmap(lambda row_key: jax.random.permutation(row_key, span))(row_keys)
    ranking = jnp.argsort(shuffled, axis=1).astype(jnp.int32)
    centre = SHARD_BLOCKS + local
    inside = (offsets[None, :] >= centre[:, None] - 1) & (offsets[None, :] <= centre[:, None] + 1)
    ordering = inside.astype(jnp.int32) * span + ranking
    strides = jnp.argsort(ordering, axis=1, stable=True)[:, :MAXB - 3].astype(jnp.int32)
    picked = jnp.concatenate([centre[:, None], centre[:, None] - 1, centre[:, None] + 1, strides], axis=1)
    global_blocks = jnp.mod(shard[:, None] * SHARD_BLOCKS - SHARD_BLOCKS + picked, QBLOCKS)
    amount = 3 + jax.random.randint(jax.random.fold_in(key, 9), (QBLOCKS,), 0, MAXB - 2)
    amount = amount.at[0].set(MAXB).at[QBLOCKS - 1].set(3)
    slot_ids = jnp.arange(MAXB, dtype=jnp.int32)
    global_blocks = jnp.where(slot_ids[None, :] < amount[:, None], global_blocks, global_blocks[:, :1])
    return (global_blocks.astype(jnp.int32), amount.astype(jnp.int32))


def draw_key_blocks(key, part):
    return block_pattern(jax.random.fold_in(key, 5))[0]


def draw_counts(key, part):
    return block_pattern(jax.random.fold_in(key, 5))[1]


def block_scale(key, dims, shards, smallest, top_value):
    level, own = 1.0, jax.random.fold_in(key, 6)
    for dim, blocks in shards:
        heights = jnp.exp(jax.random.uniform(jax.random.fold_in(own, dim), (blocks,), jnp.float32, smallest / len(shards), top_value / len(shards)))
        level = level * jnp.repeat(heights, dims[dim] // blocks).reshape([-1 if axis == dim else 1 for axis in range(len(dims))])
    return level


def scatter_about(key, extent, scale, bound, pieces=(), held_as=jnp.bfloat16):
    array = scale * jax.random.normal(key, extent, jnp.float32)
    if pieces:
        array = array * block_scale(key, extent, pieces, -0.22, 0.18)
    return jnp.clip(array, -bound, bound).astype(held_as)


def setup_inputs(seed: int = 0) -> dict:
    splits = jax.random.split(jax.random.key(seed), 6)
    queries = draw_queries(jax.random.fold_in(splits[5], 71), 0)
    keys = draw_keys(jax.random.fold_in(splits[5], 71), 0)
    values = scatter_about(splits[2], (TOKENS, D), 3.0, 15.0, ((0, 32),))
    key_blocks = draw_key_blocks(jax.random.fold_in(splits[5], 71), 0)
    counts = draw_counts(jax.random.fold_in(splits[5], 71), 0)
    return {"queries": queries, "keys": keys, "values": values, "key_blocks": key_blocks, "counts": counts}


def reference(queries, keys, values, key_blocks, counts):
    scale = HD ** -0.5
    q_blocks = queries.reshape(QBLOCKS, BLOCK, HEADS, HD)
    k_blocks = keys.reshape(QBLOCKS, BLOCK, HEADS, HD)
    v_blocks = values.reshape(QBLOCKS, BLOCK, HEADS, HD)
    slot_ids = jnp.arange(MAXB, dtype=jnp.int32)

    def attend_block(index):
        listed = key_blocks[index]
        usable = (slot_ids < counts[index])[None, None, :, None]
        query_f = q_blocks[index].astype(jnp.float32)
        key_f = k_blocks[listed].astype(jnp.float32)
        value_f = v_blocks[listed].astype(jnp.float32)
        scores = jnp.einsum('qhd,jkhd->hqjk', query_f, key_f) * scale
        top = jnp.max(jnp.where(usable, scores, -jnp.inf), axis=(2, 3), keepdims=True)
        expo = jnp.where(usable, jnp.exp(scores - top), 0.0)
        total = jnp.sum(expo, axis=(2, 3))
        weights = lax.optimization_barrier(expo.astype(jnp.bfloat16)).astype(jnp.float32)
        mixed = jnp.einsum('hqjk,jkhd->qhd', weights, value_f) / jnp.transpose(total)[:, :, None]
        return mixed.astype(jnp.bfloat16).reshape(BLOCK, D)

    result = lax.map(attend_block, jnp.arange(QBLOCKS, dtype=jnp.int32))
    return result.reshape(TOKENS, D)
```

```python
import functools
import math

import jax
import jax.numpy as jnp
from jax import lax
from jax.experimental import pallas as pl
from jax.experimental.pallas import tpu as pltpu
from jax.sharding import PartitionSpec as P

HD = 128
BLOCK = 512
MAXB = 6


def from_behind(value, axis, steps):
    count = lax.axis_size(axis)
    pairs = [(source, (source + steps) % count) for source in range(count)]
    return lax.ppermute(value, axis, pairs)


def attend_shard(query_rows, context, listed_rows, count_rows):
    scale = HD ** (-0.5)
    group_rows = query_rows.shape[0]
    heads_local = query_rows.shape[1] // HD
    blocks_here = group_rows // BLOCK
    q_blocks = query_rows.reshape(blocks_here, BLOCK, heads_local, HD)
    pair_blocks = context.reshape(2, 3 * blocks_here, BLOCK, heads_local, HD)
    slot_ids = jnp.arange(MAXB, dtype=jnp.int32)

    def attend_block(inputs):
        query_block, listed, amount = inputs
        chosen = pair_blocks[:, listed]
        usable = (slot_ids < amount)[None, None, :, None]
        scores = (
            jnp.einsum("qhd,jkhd->hqjk", query_block, chosen[0], preferred_element_type=jnp.float32)
            * scale
        )
        top = jnp.max(jnp.where(usable, scores, -jnp.inf), axis=(2, 3), keepdims=True)
        expo = jnp.where(usable, jnp.exp(scores - top), 0.0)
        total = jnp.sum(expo, axis=(2, 3))
        weights = expo.astype(jnp.bfloat16)
        mixed = jnp.einsum("hqjk,jkhd->qhd", weights, chosen[1], preferred_element_type=jnp.float32)
        mixed = mixed / jnp.transpose(total)[:, :, None]
        return mixed.astype(jnp.bfloat16).reshape(BLOCK, heads_local * HD)

    result = lax.map(attend_block, (q_blocks, listed_rows, count_rows))
    return result.reshape(group_rows, heads_local * HD)


def local(queries, keys, values, key_blocks, counts):
    cycle_size = lax.axis_size("blk")
    query_rows = lax.all_to_all(queries, "head", split_axis=1, concat_axis=0, tiled=True)
    head_pair = lax.all_to_all(
        jnp.stack([keys, values]), "head", split_axis=2, concat_axis=1, tiled=True
    )
    earlier = from_behind(head_pair, "blk", 1)
    later = from_behind(head_pair, "blk", -1)
    context = jnp.concatenate([earlier, head_pair, later], axis=1)
    blocks_here = query_rows.shape[0] // BLOCK
    total_blocks = blocks_here * cycle_size
    first_block = lax.axis_index("blk") * blocks_here
    listed_rows = lax.dynamic_slice_in_dim(key_blocks, first_block, blocks_here, 0)
    count_rows = lax.dynamic_slice_in_dim(counts, first_block, blocks_here, 0)
    local_index = jnp.mod(listed_rows - first_block + blocks_here, total_blocks)
    attended_rows = attend_shard(query_rows, context, local_index, count_rows)
    return lax.all_to_all(attended_rows, "head", split_axis=0, concat_axis=1, tiled=True)


MESH = pl.DeviceIdType.MESH
QTILE = 256


def head_kernel(
    cycle, group, blocks_here, q_ref, k_ref, v_ref, bias_ref, out_ref,
    q_all, k_all, v_all, o_all, scores, weights, total,
    send_sem, recv_sem, own_sem, out_send_sem, out_recv_sem, out_own_sem,
):
    count = cycle * group
    rows = q_ref.shape[0]
    my_blk = lax.axis_index("blk")
    my_head = lax.axis_index("head")
    me = my_blk * group + my_head
    span = 3 * blocks_here
    blocks = cycle * blocks_here
    exponent = HD ** (-0.5) * math.log2(math.e)
    inputs = ((k_ref, k_all), (q_ref, q_all), (v_ref, v_all))

    def target(step):
        blk = lax.rem(my_blk + lax.div(step, group), cycle)
        head = lax.rem(my_head + lax.rem(step, group), group)
        return blk, head

    def columns(device):
        return pl.ds(pl.multiple_of(device * HD, HD), HD)

    def rows_of(device):
        return pl.ds(pl.multiple_of(device * rows, rows), rows)

    barrier = pltpu.get_barrier_semaphore()

    def greet(step, carry):
        pl.semaphore_signal(barrier, inc=1, device_id=target(step), device_id_type=MESH)
        return carry

    lax.fori_loop(1, count, greet, 0)
    pl.semaphore_wait(barrier, count - 1)

    for index, (source, gathered) in enumerate(inputs):

        def send(step, carry):
            blk, head = target(step)
            pltpu.make_async_remote_copy(
                src_ref=source.at[:, columns(blk * group + head)],
                dst_ref=gathered.at[rows_of(me), :],
                send_sem=send_sem.at[index],
                recv_sem=recv_sem.at[index],
                device_id=(blk, head),
                device_id_type=MESH,
            ).start()
            return carry

        lax.fori_loop(1, count, send, 0)
        pltpu.make_async_copy(
            source.at[:, columns(me)], gathered.at[rows_of(me), :], own_sem.at[index]
        ).start()

    def arrived(index):
        source, gathered = inputs[index]
        pltpu.make_async_copy(
            source.at[:, columns(me)], gathered.at[rows_of(me), :], own_sem.at[index]
        ).wait()
        others = gathered.at[pl.ds(0, (count - 1) * rows), :]
        pltpu.make_async_copy(others, others, recv_sem.at[index]).wait()

    def key_rows(block, j):
        shard = lax.div(block, blocks_here)
        chosen = lax.rem((shard + cycle - 1) * blocks_here + j, blocks)
        return pl.ds(pl.multiple_of(chosen * BLOCK, BLOCK), BLOCK)

    arrived(0)
    arrived(1)
    tiles = BLOCK // QTILE

    def weigh(step, carry):
        block = lax.div(step, tiles)
        here = pl.ds(pl.multiple_of(step * QTILE, QTILE), QTILE)
        query = q_all[here, :]
        top = None
        for j in range(span):
            part = lax.dot_general(
                query, k_all[key_rows(block, j), :], (((1,), (1,)), ((), ())),
                preferred_element_type=jnp.float32,
            )
            scores[j] = part
            part_top = jnp.max(part, axis=1, keepdims=True) + bias_ref[block, j]
            top = part_top if top is None else jnp.maximum(top, part_top)
        shift = top * exponent
        amount = None
        for j in range(span):
            expo = jnp.exp2(scores[j] * exponent + (bias_ref[block, j] - shift))
            weights[here, j * BLOCK:(j + 1) * BLOCK] = expo.astype(jnp.bfloat16)
            part_sum = jnp.sum(expo, axis=1, keepdims=True)
            amount = part_sum if amount is None else amount + part_sum
        total[here, :] = amount
        return carry

    lax.fori_loop(0, blocks * tiles, weigh, 0)
    arrived(2)

    owners = BLOCK // rows
    my_block = lax.div(me, owners)
    half = blocks // 2

    def finish(step, carry):
        offset = lax.rem(2 * step + 1 + lax.div(step, half), blocks)
        block = lax.rem(my_block + offset, blocks)

        def mix(tile, inner):
            start = block * BLOCK + tile * QTILE
            here = pl.ds(pl.multiple_of(start, QTILE), QTILE)
            mixed = None
            for j in range(span):
                part = jnp.dot(
                    weights[here, j * BLOCK:(j + 1) * BLOCK], v_all[key_rows(block, j), :],
                    preferred_element_type=jnp.float32,
                )
                mixed = part if mixed is None else mixed + part
            o_all[here, :] = (mixed / total[here, :]).astype(jnp.bfloat16)
            return inner

        lax.fori_loop(0, tiles, mix, 0)

        def give(owner, inner):
            device = block * owners + owner

            @pl.when(device != me)
            def _():
                pltpu.make_async_remote_copy(
                    src_ref=o_all.at[rows_of(device), :],
                    dst_ref=out_ref.at[:, columns(me)],
                    send_sem=out_send_sem,
                    recv_sem=out_recv_sem,
                    device_id=(lax.div(device, group), lax.rem(device, group)),
                    device_id_type=MESH,
                ).start()

            @pl.when(device == me)
            def _():
                pltpu.make_async_copy(
                    o_all.at[rows_of(device), :], out_ref.at[:, columns(me)], out_own_sem
                ).start()

            return inner

        lax.fori_loop(0, owners, give, 0)
        return carry

    lax.fori_loop(0, blocks, finish, 0)

    pltpu.make_async_copy(
        o_all.at[rows_of(me), :], out_ref.at[:, columns(me)], out_own_sem
    ).wait()
    others = o_all.at[pl.ds(0, (count - 1) * rows), :]
    for index in range(3):
        pltpu.make_async_copy(others, others, send_sem.at[index]).wait()
    pltpu.make_async_copy(others, others, out_send_sem).wait()
    pltpu.make_async_copy(others, others, out_recv_sem).wait()


def local_heads(cycle, group, queries, keys, values, key_blocks, counts):
    rows, width = queries.shape
    tokens = rows * cycle * group
    blocks = tokens // BLOCK
    blocks_here = blocks // cycle
    span = 3 * blocks_here
    block_ids = jnp.arange(blocks, dtype=jnp.int32)
    first = (block_ids // blocks_here + cycle - 1) * blocks_here
    offered = (first[:, None] + jnp.arange(span, dtype=jnp.int32)[None, :]) % blocks
    used = jnp.arange(key_blocks.shape[1], dtype=jnp.int32)[None, :] < counts[:, None]
    listed = (key_blocks[:, None, :] == offered[:, :, None]) & used[:, None, :]
    bias = jnp.where(jnp.any(listed, axis=2), 0.0, -jnp.inf).astype(jnp.float32)
    whole = pltpu.VMEM((tokens, HD), jnp.bfloat16)
    return pl.pallas_call(
        functools.partial(head_kernel, cycle, group, blocks_here),
        out_shape=jax.ShapeDtypeStruct((rows, width), jnp.bfloat16),
        in_specs=[pl.BlockSpec(memory_space=pl.ANY)] * 3
        + [pl.BlockSpec(memory_space=pltpu.SMEM)],
        out_specs=pl.BlockSpec(memory_space=pl.ANY),
        scratch_shapes=[
            whole, whole, whole, whole,
            pltpu.VMEM((span, QTILE, BLOCK), jnp.float32),
            pltpu.VMEM((tokens, span * BLOCK), jnp.bfloat16),
            pltpu.VMEM((tokens, 1), jnp.float32),
            pltpu.SemaphoreType.DMA((3,)),
            pltpu.SemaphoreType.DMA((3,)),
            pltpu.SemaphoreType.DMA((3,)),
            pltpu.SemaphoreType.DMA,
            pltpu.SemaphoreType.DMA,
            pltpu.SemaphoreType.DMA,
        ],
        compiler_params=pltpu.CompilerParams(
            collective_id=0, has_side_effects=True, vmem_limit_bytes=56 * 2**20
        ),
        cost_estimate=pl.CostEstimate(
            flops=4 * tokens * span * BLOCK * HD,
            bytes_accessed=8 * rows * width,
            transcendentals=tokens * span * BLOCK,
        ),
    )(queries, keys, values, bias)


def solution(mesh):
    cycle, group = mesh.shape["blk"], mesh.shape["head"]
    placed = (
        P(("blk", "head"), None),
        P(("blk", "head"), None),
        P(("blk", "head"), None),
        P(),
        P(),
    )
    one_head_each = cycle * group * HD

    def chosen(queries, *others):
        if queries.shape[1] == one_head_each and cycle >= 3:
            return local_heads(cycle, group, queries, *others)
        return local(queries, *others)

    return jax.shard_map(
        chosen, mesh=mesh, in_specs=placed, out_specs=P(("blk", "head"), None), check_vma=False
    )
```

```python
import functools
import math

import jax
import jax.numpy as jnp
from jax import lax
from jax.experimental import pallas as pl
from jax.experimental.pallas import tpu as pltpu
from jax.sharding import PartitionSpec as P

HD = 128
BLOCK = 512
MAXB = 6


def from_behind(value, axis, steps):
    count = lax.axis_size(axis)
    pairs = [(source, (source + steps) % count) for source in range(count)]
    return lax.ppermute(value, axis, pairs)


def attend_shard(query_rows, context, listed_rows, count_rows):
    scale = HD ** (-0.5)
    group_rows = query_rows.shape[0]
    heads_local = query_rows.shape[1] // HD
    blocks_here = group_rows // BLOCK
    q_blocks = query_rows.reshape(blocks_here, BLOCK, heads_local, HD)
    pair_blocks = context.reshape(2, 3 * blocks_here, BLOCK, heads_local, HD)
    slot_ids = jnp.arange(MAXB, dtype=jnp.int32)

    def attend_block(inputs):
        query_block, listed, amount = inputs
        chosen = pair_blocks[:, listed]
        usable = (slot_ids < amount)[None, None, :, None]
        scores = (
            jnp.einsum("qhd,jkhd->hqjk", query_block, chosen[0], preferred_element_type=jnp.float32)
            * scale
        )
        top = jnp.max(jnp.where(usable, scores, -jnp.inf), axis=(2, 3), keepdims=True)
        expo = jnp.where(usable, jnp.exp(scores - top), 0.0)
        total = jnp.sum(expo, axis=(2, 3))
        weights = expo.astype(jnp.bfloat16)
        mixed = jnp.einsum("hqjk,jkhd->qhd", weights, chosen[1], preferred_element_type=jnp.float32)
        mixed = mixed / jnp.transpose(total)[:, :, None]
        return mixed.astype(jnp.bfloat16).reshape(BLOCK, heads_local * HD)

    result = lax.map(attend_block, (q_blocks, listed_rows, count_rows))
    return result.reshape(group_rows, heads_local * HD)


def local(queries, keys, values, key_blocks, counts):
    cycle_size = lax.axis_size("blk")
    query_rows = lax.all_to_all(queries, "head", split_axis=1, concat_axis=0, tiled=True)
    head_pair = lax.all_to_all(
        jnp.stack([keys, values]), "head", split_axis=2, concat_axis=1, tiled=True
    )
    earlier = from_behind(head_pair, "blk", 1)
    later = from_behind(head_pair, "blk", -1)
    context = jnp.concatenate([earlier, head_pair, later], axis=1)
    blocks_here = query_rows.shape[0] // BLOCK
    total_blocks = blocks_here * cycle_size
    first_block = lax.axis_index("blk") * blocks_here
    listed_rows = lax.dynamic_slice_in_dim(key_blocks, first_block, blocks_here, 0)
    count_rows = lax.dynamic_slice_in_dim(counts, first_block, blocks_here, 0)
    local_index = jnp.mod(listed_rows - first_block + blocks_here, total_blocks)
    attended_rows = attend_shard(query_rows, context, local_index, count_rows)
    return lax.all_to_all(attended_rows, "head", split_axis=0, concat_axis=1, tiled=True)


MESH = pl.DeviceIdType.MESH
QTILE = 256


def head_kernel(
    cycle, group, blocks_here, q_ref, k_ref, v_ref, lists_ref, counts_ref, out_ref,
    q_all, k_all, v_all, o_all, scores, weights, total, lists, amounts, bias_ref,
    send_sem, recv_sem, own_sem, list_sem, out_send_sem, out_recv_sem, out_own_sem,
):
    count = cycle * group
    rows = q_ref.shape[0]
    my_blk = lax.axis_index("blk")
    my_head = lax.axis_index("head")
    me = my_blk * group + my_head
    span = 3 * blocks_here
    blocks = cycle * blocks_here
    exponent = HD ** (-0.5) * math.log2(math.e)
    inputs = ((k_ref, k_all), (q_ref, q_all), (v_ref, v_all))

    def target(step):
        blk = lax.rem(my_blk + lax.div(step, group), cycle)
        head = lax.rem(my_head + lax.rem(step, group), group)
        return blk, head

    def columns(device):
        return pl.ds(pl.multiple_of(device * HD, HD), HD)

    def rows_of(device):
        return pl.ds(pl.multiple_of(device * rows, rows), rows)

    barrier = pltpu.get_barrier_semaphore()

    def greet(step, carry):
        pl.semaphore_signal(barrier, inc=1, device_id=target(step), device_id_type=MESH)
        return carry

    lax.fori_loop(1, count, greet, 0)
    pl.semaphore_wait(barrier, count - 1)

    def send_all(index):
        source, gathered = inputs[index]

        def send(step, carry):
            blk, head = target(step)
            pltpu.make_async_remote_copy(
                src_ref=source.at[:, columns(blk * group + head)],
                dst_ref=gathered.at[rows_of(me), :],
                send_sem=send_sem.at[index],
                recv_sem=recv_sem.at[index, lax.div(step, group)],
                device_id=(blk, head),
                device_id_type=MESH,
            ).start()
            return carry

        lax.fori_loop(1, count, send, 0)

    def own_copy(index):
        source, gathered = inputs[index]
        return pltpu.make_async_copy(
            source.at[:, columns(me)], gathered.at[rows_of(me), :], own_sem.at[index]
        )

    def arrived(index, back):
        gathered = inputs[index][1]
        if back == 0:
            own_copy(index).wait()
        senders = group - 1 if back == 0 else group
        part = gathered.at[pl.ds(0, senders * rows), :]
        pltpu.make_async_copy(part, part, recv_sem.at[index, back]).wait()

    def key_block(block, j):
        shard = lax.div(block, blocks_here)
        return lax.rem((shard + cycle - 1) * blocks_here + j, blocks)

    def key_rows(block, j):
        return pl.ds(pl.multiple_of(key_block(block, j) * BLOCK, BLOCK), BLOCK)

    send_all(0)
    send_all(1)
    for index in range(3):
        own_copy(index).start()
    list_copies = (
        pltpu.make_async_copy(lists_ref, lists, list_sem.at[0]),
        pltpu.make_async_copy(counts_ref, amounts, list_sem.at[1]),
    )
    for copy in list_copies:
        copy.start()
    for copy in list_copies:
        copy.wait()

    def mark(block, carry):
        for j in range(span):
            offered = key_block(block, j)
            hits = jnp.int32(0)
            for slot in range(MAXB):
                same = lists[block, slot] == offered
                hits += jnp.where(same & (slot < amounts[block]), 1, 0)
            bias_ref[block, j] = jnp.where(hits > 0, 0.0, -jnp.inf)
        return carry

    lax.fori_loop(0, blocks, mark, 0)

    for back in range(cycle):
        arrived(0, back)
    send_all(2)
    tiles = BLOCK // QTILE

    def weigh(step, carry):
        block = lax.div(step, tiles)
        here = pl.ds(pl.multiple_of(step * QTILE, QTILE), QTILE)
        query = q_all[here, :]
        top = None
        for j in range(span):
            part = lax.dot_general(
                query, k_all[key_rows(block, j), :], (((1,), (1,)), ((), ())),
                preferred_element_type=jnp.float32,
            )
            scores[j] = part
            part_top = jnp.max(part, axis=1, keepdims=True) + bias_ref[block, j]
            top = part_top if top is None else jnp.maximum(top, part_top)
        shift = top * exponent
        amount = None
        for j in range(span):
            expo = jnp.exp2(scores[j] * exponent + (bias_ref[block, j] - shift))
            weights[here, j * BLOCK:(j + 1) * BLOCK] = expo.astype(jnp.bfloat16)
            part_sum = jnp.sum(expo, axis=1, keepdims=True)
            amount = part_sum if amount is None else amount + part_sum
        total[here, :] = amount
        return carry

    per_shard = blocks_here * tiles
    for back in range(cycle):
        arrived(1, back)
        first = lax.rem(my_blk + cycle - back, cycle) * per_shard

        def weigh_here(step, carry):
            return weigh(first + step, carry)

        lax.fori_loop(0, per_shard, weigh_here, 0)

    owners = QTILE // rows
    my_place = lax.rem(lax.div(me * rows, BLOCK), blocks_here)

    def finish(shard, turn):
        block = shard * blocks_here + lax.rem(my_place + 1 + turn, blocks_here)

        def mix(tile, inner):
            start = block * BLOCK + tile * QTILE
            here = pl.ds(pl.multiple_of(start, QTILE), QTILE)
            mixed = None
            for j in range(span):
                part = jnp.dot(
                    weights[here, j * BLOCK:(j + 1) * BLOCK], v_all[key_rows(block, j), :],
                    preferred_element_type=jnp.float32,
                )
                mixed = part if mixed is None else mixed + part
            o_all[here, :] = (mixed / total[here, :]).astype(jnp.bfloat16)

            def give(owner, carry):
                device = (block * tiles + tile) * owners + owner

                @pl.when(device != me)
                def _():
                    pltpu.make_async_remote_copy(
                        src_ref=o_all.at[rows_of(device), :],
                        dst_ref=out_ref.at[:, columns(me)],
                        send_sem=out_send_sem,
                        recv_sem=out_recv_sem,
                        device_id=(lax.div(device, group), lax.rem(device, group)),
                        device_id_type=MESH,
                    ).start()

                @pl.when(device == me)
                def _():
                    pltpu.make_async_copy(
                        o_all.at[rows_of(device), :], out_ref.at[:, columns(me)], out_own_sem
                    ).start()

                return carry

            return lax.fori_loop(0, owners, give, inner)

        lax.fori_loop(0, tiles, mix, 0)

    for back in range(3):
        arrived(2, back)

    def finish_previous(turn, carry):
        finish(lax.rem(my_blk + cycle - 1, cycle), turn)
        return carry

    lax.fori_loop(0, blocks_here, finish_previous, 0)
    for back in range(3, cycle):
        arrived(2, back)

    def finish_rest(step, carry):
        ahead = lax.rem(lax.rem(step, cycle - 1) + 1, cycle - 1)
        finish(lax.rem(my_blk + ahead, cycle), lax.div(step, cycle - 1))
        return carry

    lax.fori_loop(0, blocks_here * (cycle - 1), finish_rest, 0)

    pltpu.make_async_copy(
        o_all.at[rows_of(me), :], out_ref.at[:, columns(me)], out_own_sem
    ).wait()
    others = o_all.at[pl.ds(0, (count - 1) * rows), :]
    for index in range(3):
        pltpu.make_async_copy(others, others, send_sem.at[index]).wait()
    pltpu.make_async_copy(others, others, out_send_sem).wait()
    pltpu.make_async_copy(others, others, out_recv_sem).wait()


def local_heads(cycle, group, queries, keys, values, key_blocks, counts):
    rows, width = queries.shape
    tokens = rows * cycle * group
    blocks = tokens // BLOCK
    blocks_here = blocks // cycle
    span = 3 * blocks_here
    span = 3 * blocks_here
    whole = pltpu.VMEM((tokens, HD), jnp.bfloat16)
    return pl.pallas_call(
        functools.partial(head_kernel, cycle, group, blocks_here),
        out_shape=jax.ShapeDtypeStruct((rows, width), jnp.bfloat16),
        in_specs=[pl.BlockSpec(memory_space=pl.ANY)] * 5,
        out_specs=pl.BlockSpec(memory_space=pl.ANY),
        scratch_shapes=[
            whole, whole, whole, whole,
            pltpu.VMEM((span, QTILE, BLOCK), jnp.float32),
            pltpu.VMEM((tokens, span * BLOCK), jnp.bfloat16),
            pltpu.VMEM((tokens, 1), jnp.float32),
            pltpu.SMEM(key_blocks.shape, jnp.int32),
            pltpu.SMEM(counts.shape, jnp.int32),
            pltpu.SMEM((blocks, span), jnp.float32),
            pltpu.SemaphoreType.DMA((3,)),
            pltpu.SemaphoreType.DMA((3, cycle)),
            pltpu.SemaphoreType.DMA((3,)),
            pltpu.SemaphoreType.DMA((2,)),
            pltpu.SemaphoreType.DMA,
            pltpu.SemaphoreType.DMA,
            pltpu.SemaphoreType.DMA,
        ],
        compiler_params=pltpu.CompilerParams(
            collective_id=0, has_side_effects=True, vmem_limit_bytes=56 * 2**20
        ),
        cost_estimate=pl.CostEstimate(
            flops=4 * tokens * span * BLOCK * HD,
            bytes_accessed=8 * rows * width,
            transcendentals=tokens * span * BLOCK,
        ),
    )(queries, keys, values, key_blocks, counts)


def solution(mesh):
    cycle, group = mesh.shape["blk"], mesh.shape["head"]
    placed = (
        P(("blk", "head"), None),
        P(("blk", "head"), None),
        P(("blk", "head"), None),
        P(),
        P(),
    )
    one_head_each = cycle * group * HD

    def chosen(queries, *others):
        rows = queries.shape[0]
        aligned = QTILE % rows == 0 and rows * group % BLOCK == 0
        if queries.shape[1] == one_head_each and cycle >= 3 and aligned:
            return local_heads(cycle, group, queries, *others)
        return local(queries, *others)

    return jax.shard_map(
        chosen, mesh=mesh, in_specs=placed, out_specs=P(("blk", "head"), None), check_vma=False
    )
```

```python
import functools
import math

import jax
import jax.numpy as jnp
from jax import lax
from jax.experimental import pallas as pl
from jax.experimental.pallas import tpu as pltpu
from jax.sharding import PartitionSpec as P

HD = 128
BLOCK = 512
MAXB = 6


def from_behind(value, axis, steps):
    count = lax.axis_size(axis)
    pairs = [(source, (source + steps) % count) for source in range(count)]
    return lax.ppermute(value, axis, pairs)


def attend_shard(query_rows, context, listed_rows, count_rows):
    scale = HD ** (-0.5)
    group_rows = query_rows.shape[0]
    heads_local = query_rows.shape[1] // HD
    blocks_here = group_rows // BLOCK
    q_blocks = query_rows.reshape(blocks_here, BLOCK, heads_local, HD)
    pair_blocks = context.reshape(2, 3 * blocks_here, BLOCK, heads_local, HD)
    slot_ids = jnp.arange(MAXB, dtype=jnp.int32)

    def attend_block(inputs):
        query_block, listed, amount = inputs
        chosen = pair_blocks[:, listed]
        usable = (slot_ids < amount)[None, None, :, None]
        scores = (
            jnp.einsum("qhd,jkhd->hqjk", query_block, chosen[0], preferred_element_type=jnp.float32)
            * scale
        )
        top = jnp.max(jnp.where(usable, scores, -jnp.inf), axis=(2, 3), keepdims=True)
        expo = jnp.where(usable, jnp.exp(scores - top), 0.0)
        total = jnp.sum(expo, axis=(2, 3))
        weights = expo.astype(jnp.bfloat16)
        mixed = jnp.einsum("hqjk,jkhd->qhd", weights, chosen[1], preferred_element_type=jnp.float32)
        mixed = mixed / jnp.transpose(total)[:, :, None]
        return mixed.astype(jnp.bfloat16).reshape(BLOCK, heads_local * HD)

    result = lax.map(attend_block, (q_blocks, listed_rows, count_rows))
    return result.reshape(group_rows, heads_local * HD)


def local(queries, keys, values, key_blocks, counts):
    cycle_size = lax.axis_size("blk")
    query_rows = lax.all_to_all(queries, "head", split_axis=1, concat_axis=0, tiled=True)
    head_pair = lax.all_to_all(
        jnp.stack([keys, values]), "head", split_axis=2, concat_axis=1, tiled=True
    )
    earlier = from_behind(head_pair, "blk", 1)
    later = from_behind(head_pair, "blk", -1)
    context = jnp.concatenate([earlier, head_pair, later], axis=1)
    blocks_here = query_rows.shape[0] // BLOCK
    total_blocks = blocks_here * cycle_size
    first_block = lax.axis_index("blk") * blocks_here
    listed_rows = lax.dynamic_slice_in_dim(key_blocks, first_block, blocks_here, 0)
    count_rows = lax.dynamic_slice_in_dim(counts, first_block, blocks_here, 0)
    local_index = jnp.mod(listed_rows - first_block + blocks_here, total_blocks)
    attended_rows = attend_shard(query_rows, context, local_index, count_rows)
    return lax.all_to_all(attended_rows, "head", split_axis=0, concat_axis=1, tiled=True)


MESH = pl.DeviceIdType.MESH
QTILE = 256


def head_kernel(
    cycle, group, blocks_here, q_ref, k_ref, v_ref, lists_ref, counts_ref, out_ref,
    q_all, k_all, v_all, o_all, scores, weights, total, lists, amounts, bias_ref,
    send_sem, recv_sem, own_sem, list_sem, out_send_sem, out_recv_sem, out_own_sem,
):
    count = cycle * group
    rows = q_ref.shape[0]
    my_blk = lax.axis_index("blk")
    my_head = lax.axis_index("head")
    me = my_blk * group + my_head
    span = 3 * blocks_here
    blocks = cycle * blocks_here
    exponent = HD ** (-0.5) * math.log2(math.e)
    inputs = ((k_ref, k_all), (q_ref, q_all), (v_ref, v_all))

    def target(step):
        place = lax.rem(step, group)
        ahead = lax.div(place, 2) + (1 - lax.rem(place, 2)) * (group // 2)
        blk = lax.rem(my_blk + lax.div(step, group), cycle)
        head = lax.rem(my_head + ahead, group)
        return blk, head

    def each_partner(body):
        body(0, 0)
        lax.fori_loop(2, count, body, 0)

    def columns(device):
        return pl.ds(pl.multiple_of(device * HD, HD), HD)

    def rows_of(device):
        return pl.ds(pl.multiple_of(device * rows, rows), rows)

    barrier = pltpu.get_barrier_semaphore()

    def greet(step, carry):
        pl.semaphore_signal(barrier, inc=1, device_id=target(step), device_id_type=MESH)
        return carry

    each_partner(greet)
    pl.semaphore_wait(barrier, count - 1)

    def send_all(index):
        source, gathered = inputs[index]

        def send(step, carry):
            blk, head = target(step)
            pltpu.make_async_remote_copy(
                src_ref=source.at[:, columns(blk * group + head)],
                dst_ref=gathered.at[rows_of(me), :],
                send_sem=send_sem.at[index],
                recv_sem=recv_sem.at[index, lax.div(step, group)],
                device_id=(blk, head),
                device_id_type=MESH,
            ).start()
            return carry

        each_partner(send)

    def own_copy(index):
        source, gathered = inputs[index]
        return pltpu.make_async_copy(
            source.at[:, columns(me)], gathered.at[rows_of(me), :], own_sem.at[index]
        )

    def arrived(index, back):
        gathered = inputs[index][1]
        if back == 0:
            own_copy(index).wait()
        senders = group - 1 if back == 0 else group
        part = gathered.at[pl.ds(0, senders * rows), :]
        pltpu.make_async_copy(part, part, recv_sem.at[index, back]).wait()

    def key_block(block, j):
        shard = lax.div(block, blocks_here)
        return lax.rem((shard + cycle - 1) * blocks_here + j, blocks)

    def key_rows(block, j):
        return pl.ds(pl.multiple_of(key_block(block, j) * BLOCK, BLOCK), BLOCK)

    send_all(0)
    send_all(1)
    for index in range(3):
        own_copy(index).start()
    list_copies = (
        pltpu.make_async_copy(lists_ref, lists, list_sem.at[0]),
        pltpu.make_async_copy(counts_ref, amounts, list_sem.at[1]),
    )
    for copy in list_copies:
        copy.start()
    for copy in list_copies:
        copy.wait()

    def mark(block, carry):
        for j in range(span):
            offered = key_block(block, j)
            hits = jnp.int32(0)
            for slot in range(MAXB):
                same = lists[block, slot] == offered
                hits += jnp.where(same & (slot < amounts[block]), 1, 0)
            bias_ref[block, j] = jnp.where(hits > 0, 0.0, -jnp.inf)
        return carry

    lax.fori_loop(0, blocks, mark, 0)

    for back in range(cycle):
        arrived(0, back)
    send_all(2)
    tiles = BLOCK // QTILE

    def weigh(step, carry):
        block = lax.div(step, tiles)
        here = pl.ds(pl.multiple_of(step * QTILE, QTILE), QTILE)
        query = q_all[here, :]
        top = None
        for j in range(span):
            part = lax.dot_general(
                query, k_all[key_rows(block, j), :], (((1,), (1,)), ((), ())),
                preferred_element_type=jnp.float32,
            )
            scores[j] = part
            part_top = jnp.max(part, axis=1, keepdims=True) + bias_ref[block, j]
            top = part_top if top is None else jnp.maximum(top, part_top)
        shift = top * exponent
        amount = None
        for j in range(span):
            expo = jnp.exp2(scores[j] * exponent + (bias_ref[block, j] - shift))
            weights[here, j * BLOCK:(j + 1) * BLOCK] = expo.astype(jnp.bfloat16)
            part_sum = jnp.sum(expo, axis=1, keepdims=True)
            amount = part_sum if amount is None else amount + part_sum
        total[here, :] = amount
        return carry

    per_shard = blocks_here * tiles
    for back in range(cycle):
        arrived(1, back)
        first = lax.rem(my_blk + cycle - back, cycle) * per_shard

        def weigh_here(step, carry):
            return weigh(first + step, carry)

        lax.fori_loop(0, per_shard, weigh_here, 0)

    owners = QTILE // rows
    my_place = lax.rem(lax.div(me * rows, BLOCK), blocks_here)

    def finish(shard, turn):
        block = shard * blocks_here + lax.rem(my_place + 1 + turn, blocks_here)

        def mix(tile, inner):
            start = block * BLOCK + tile * QTILE
            here = pl.ds(pl.multiple_of(start, QTILE), QTILE)
            mixed = None
            for j in range(span):
                part = jnp.dot(
                    weights[here, j * BLOCK:(j + 1) * BLOCK], v_all[key_rows(block, j), :],
                    preferred_element_type=jnp.float32,
                )
                mixed = part if mixed is None else mixed + part
            o_all[here, :] = (mixed / total[here, :]).astype(jnp.bfloat16)

            def give(owner, carry):
                device = (block * tiles + tile) * owners + owner

                @pl.when(device != me)
                def _():
                    pltpu.make_async_remote_copy(
                        src_ref=o_all.at[rows_of(device), :],
                        dst_ref=out_ref.at[:, columns(me)],
                        send_sem=out_send_sem,
                        recv_sem=out_recv_sem,
                        device_id=(lax.div(device, group), lax.rem(device, group)),
                        device_id_type=MESH,
                    ).start()

                @pl.when(device == me)
                def _():
                    pltpu.make_async_copy(
                        o_all.at[rows_of(device), :], out_ref.at[:, columns(me)], out_own_sem
                    ).start()

                return carry

            return lax.fori_loop(0, owners, give, inner)

        lax.fori_loop(0, tiles, mix, 0)

    for back in range(3):
        arrived(2, back)

    def finish_previous(turn, carry):
        finish(lax.rem(my_blk + cycle - 1, cycle), turn)
        return carry

    lax.fori_loop(0, blocks_here, finish_previous, 0)
    for back in range(3, cycle):
        arrived(2, back)

    def finish_rest(step, carry):
        ahead = lax.rem(lax.rem(step, cycle - 1) + 1, cycle - 1)
        finish(lax.rem(my_blk + ahead, cycle), lax.div(step, cycle - 1))
        return carry

    lax.fori_loop(0, blocks_here * (cycle - 1), finish_rest, 0)

    pltpu.make_async_copy(
        o_all.at[rows_of(me), :], out_ref.at[:, columns(me)], out_own_sem
    ).wait()
    others = o_all.at[pl.ds(0, (count - 1) * rows), :]
    for index in range(3):
        pltpu.make_async_copy(others, others, send_sem.at[index]).wait()
    pltpu.make_async_copy(others, others, out_send_sem).wait()
    pltpu.make_async_copy(others, others, out_recv_sem).wait()


def local_heads(cycle, group, queries, keys, values, key_blocks, counts):
    rows, width = queries.shape
    tokens = rows * cycle * group
    blocks = tokens // BLOCK
    blocks_here = blocks // cycle
    span = 3 * blocks_here
    span = 3 * blocks_here
    whole = pltpu.VMEM((tokens, HD), jnp.bfloat16)
    return pl.pallas_call(
        functools.partial(head_kernel, cycle, group, blocks_here),
        out_shape=jax.ShapeDtypeStruct((rows, width), jnp.bfloat16),
        in_specs=[pl.BlockSpec(memory_space=pl.ANY)] * 5,
        out_specs=pl.BlockSpec(memory_space=pl.ANY),
        scratch_shapes=[
            whole, whole, whole, whole,
            pltpu.VMEM((span, QTILE, BLOCK), jnp.float32),
            pltpu.VMEM((tokens, span * BLOCK), jnp.bfloat16),
            pltpu.VMEM((tokens, 1), jnp.float32),
            pltpu.SMEM(key_blocks.shape, jnp.int32),
            pltpu.SMEM(counts.shape, jnp.int32),
            pltpu.SMEM((blocks, span), jnp.float32),
            pltpu.SemaphoreType.DMA((3,)),
            pltpu.SemaphoreType.DMA((3, cycle)),
            pltpu.SemaphoreType.DMA((3,)),
            pltpu.SemaphoreType.DMA((2,)),
            pltpu.SemaphoreType.DMA,
            pltpu.SemaphoreType.DMA,
            pltpu.SemaphoreType.DMA,
        ],
        compiler_params=pltpu.CompilerParams(
            collective_id=0, has_side_effects=True, vmem_limit_bytes=56 * 2**20
        ),
        cost_estimate=pl.CostEstimate(
            flops=4 * tokens * span * BLOCK * HD,
            bytes_accessed=8 * rows * width,
            transcendentals=tokens * span * BLOCK,
        ),
    )(queries, keys, values, key_blocks, counts)


def solution(mesh):
    cycle, group = mesh.shape["blk"], mesh.shape["head"]
    placed = (
        P(("blk", "head"), None),
        P(("blk", "head"), None),
        P(("blk", "head"), None),
        P(),
        P(),
    )
    one_head_each = cycle * group * HD

    def chosen(queries, *others):
        rows = queries.shape[0]
        aligned = QTILE % rows == 0 and rows * group % BLOCK == 0
        if queries.shape[1] == one_head_each and cycle >= 3 and group % 2 == 0 and aligned:
            return local_heads(cycle, group, queries, *others)
        return local(queries, *others)

    return jax.shard_map(
        chosen, mesh=mesh, in_specs=placed, out_specs=P(("blk", "head"), None), check_vma=False
    )
```

```python
import functools
import math

import jax
import jax.numpy as jnp
from jax import lax
from jax.experimental import pallas as pl
from jax.experimental.pallas import tpu as pltpu
from jax.sharding import PartitionSpec as P

HD = 128
BLOCK = 512
MAXB = 6


def from_behind(value, axis, steps):
    count = lax.axis_size(axis)
    pairs = [(source, (source + steps) % count) for source in range(count)]
    return lax.ppermute(value, axis, pairs)


def attend_shard(query_rows, context, listed_rows, count_rows):
    scale = HD ** (-0.5)
    group_rows = query_rows.shape[0]
    heads_local = query_rows.shape[1] // HD
    blocks_here = group_rows // BLOCK
    q_blocks = query_rows.reshape(blocks_here, BLOCK, heads_local, HD)
    pair_blocks = context.reshape(2, 3 * blocks_here, BLOCK, heads_local, HD)
    slot_ids = jnp.arange(MAXB, dtype=jnp.int32)

    def attend_block(inputs):
        query_block, listed, amount = inputs
        chosen = pair_blocks[:, listed]
        usable = (slot_ids < amount)[None, None, :, None]
        scores = (
            jnp.einsum("qhd,jkhd->hqjk", query_block, chosen[0], preferred_element_type=jnp.float32)
            * scale
        )
        top = jnp.max(jnp.where(usable, scores, -jnp.inf), axis=(2, 3), keepdims=True)
        expo = jnp.where(usable, jnp.exp(scores - top), 0.0)
        total = jnp.sum(expo, axis=(2, 3))
        weights = expo.astype(jnp.bfloat16)
        mixed = jnp.einsum("hqjk,jkhd->qhd", weights, chosen[1], preferred_element_type=jnp.float32)
        mixed = mixed / jnp.transpose(total)[:, :, None]
        return mixed.astype(jnp.bfloat16).reshape(BLOCK, heads_local * HD)

    result = lax.map(attend_block, (q_blocks, listed_rows, count_rows))
    return result.reshape(group_rows, heads_local * HD)


def local(queries, keys, values, key_blocks, counts):
    cycle_size = lax.axis_size("blk")
    query_rows = lax.all_to_all(queries, "head", split_axis=1, concat_axis=0, tiled=True)
    head_pair = lax.all_to_all(
        jnp.stack([keys, values]), "head", split_axis=2, concat_axis=1, tiled=True
    )
    earlier = from_behind(head_pair, "blk", 1)
    later = from_behind(head_pair, "blk", -1)
    context = jnp.concatenate([earlier, head_pair, later], axis=1)
    blocks_here = query_rows.shape[0] // BLOCK
    total_blocks = blocks_here * cycle_size
    first_block = lax.axis_index("blk") * blocks_here
    listed_rows = lax.dynamic_slice_in_dim(key_blocks, first_block, blocks_here, 0)
    count_rows = lax.dynamic_slice_in_dim(counts, first_block, blocks_here, 0)
    local_index = jnp.mod(listed_rows - first_block + blocks_here, total_blocks)
    attended_rows = attend_shard(query_rows, context, local_index, count_rows)
    return lax.all_to_all(attended_rows, "head", split_axis=0, concat_axis=1, tiled=True)


MESH = pl.DeviceIdType.MESH
QTILE = 256


def head_kernel(
    cycle, group, blocks_here, q_ref, k_ref, v_ref, lists_ref, counts_ref, out_ref,
    q_all, k_all, v_all, o_all, scores, weights, total, lists, amounts, bias_ref,
    send_sem, recv_sem, own_sem, list_sem, out_send_sem, out_recv_sem, out_own_sem,
):
    count = cycle * group
    rows = q_ref.shape[0]
    my_blk = lax.axis_index("blk")
    my_head = lax.axis_index("head")
    me = my_blk * group + my_head
    span = 3 * blocks_here
    blocks = cycle * blocks_here
    exponent = HD ** (-0.5) * math.log2(math.e)
    inputs = ((k_ref, k_all), (q_ref, q_all), (v_ref, v_all))

    def target(step):
        place = lax.rem(step, group)
        ahead = lax.div(place, 2) + (1 - lax.rem(place, 2)) * (group // 2)
        blk = lax.rem(my_blk + lax.div(step, group), cycle)
        head = lax.rem(my_head + ahead, group)
        return blk, head

    def columns(device):
        return pl.ds(pl.multiple_of(device * HD, HD), HD)

    def rows_of(device):
        return pl.ds(pl.multiple_of(device * rows, rows), rows)

    barrier = pltpu.get_barrier_semaphore()

    for step in range(count):
        if step != 1:
            pl.semaphore_signal(barrier, inc=1, device_id=target(step), device_id_type=MESH)
    pl.semaphore_wait(barrier, count - 1)

    def send_group(index, back):
        source, gathered = inputs[index]

        def send(step, carry):
            blk, head = target(step)
            pltpu.make_async_remote_copy(
                src_ref=source.at[:, columns(blk * group + head)],
                dst_ref=gathered.at[rows_of(me), :],
                send_sem=send_sem.at[index],
                recv_sem=recv_sem.at[index, back],
                device_id=(blk, head),
                device_id_type=MESH,
            ).start()
            return carry

        if back == 0:
            send(0, 0)
            lax.fori_loop(2, group, send, 0)
        else:
            lax.fori_loop(back * group, (back + 1) * group, send, 0)

    def own_copy(index):
        source, gathered = inputs[index]
        return pltpu.make_async_copy(
            source.at[:, columns(me)], gathered.at[rows_of(me), :], own_sem.at[index]
        )

    def arrived(index, back):
        gathered = inputs[index][1]
        if back == 0:
            own_copy(index).wait()
        senders = group - 1 if back == 0 else group
        part = gathered.at[pl.ds(0, senders * rows), :]
        pltpu.make_async_copy(part, part, recv_sem.at[index, back]).wait()

    def key_block(block, j):
        shard = lax.div(block, blocks_here)
        return lax.rem((shard + cycle - 1) * blocks_here + j, blocks)

    def key_rows(block, j):
        return pl.ds(pl.multiple_of(key_block(block, j) * BLOCK, BLOCK), BLOCK)

    later = (0,) + tuple(range(2, cycle))
    for back in range(3):
        send_group(0, back)
    send_group(1, 1)
    for back in range(3, cycle):
        send_group(0, back)
    for back in later:
        send_group(1, back)
    for index in range(3):
        own_copy(index).start()
    list_copies = (
        pltpu.make_async_copy(lists_ref, lists, list_sem.at[0]),
        pltpu.make_async_copy(counts_ref, amounts, list_sem.at[1]),
    )
    for copy in list_copies:
        copy.start()
    for copy in list_copies:
        copy.wait()

    def mark(block, carry):
        for j in range(span):
            offered = key_block(block, j)
            hits = jnp.int32(0)
            for slot in range(MAXB):
                same = lists[block, slot] == offered
                hits += jnp.where(same & (slot < amounts[block]), 1, 0)
            bias_ref[block, j] = jnp.where(hits > 0, 0.0, -jnp.inf)
        return carry

    lax.fori_loop(0, blocks, mark, 0)

    for back in range(3):
        arrived(0, back)
    for back in range(cycle):
        send_group(2, back)
    tiles = BLOCK // QTILE

    def weigh(step, carry):
        block = lax.div(step, tiles)
        here = pl.ds(pl.multiple_of(step * QTILE, QTILE), QTILE)
        query = q_all[here, :]
        top = None
        for j in range(span):
            part = lax.dot_general(
                query, k_all[key_rows(block, j), :], (((1,), (1,)), ((), ())),
                preferred_element_type=jnp.float32,
            )
            scores[j] = part
            part_top = jnp.max(part, axis=1, keepdims=True) + bias_ref[block, j]
            top = part_top if top is None else jnp.maximum(top, part_top)
        shift = top * exponent
        amount = None
        for j in range(span):
            expo = jnp.exp2(scores[j] * exponent + (bias_ref[block, j] - shift))
            weights[here, j * BLOCK:(j + 1) * BLOCK] = expo.astype(jnp.bfloat16)
            part_sum = jnp.sum(expo, axis=1, keepdims=True)
            amount = part_sum if amount is None else amount + part_sum
        total[here, :] = amount
        return carry

    per_shard = blocks_here * tiles
    def weigh_shard(back):
        arrived(1, back)
        first = lax.rem(my_blk + cycle - back, cycle) * per_shard

        def weigh_here(step, carry):
            return weigh(first + step, carry)

        lax.fori_loop(0, per_shard, weigh_here, 0)

    weigh_shard(1)
    for back in range(3, cycle):
        arrived(0, back)
    for back in later:
        weigh_shard(back)

    owners = QTILE // rows
    my_place = lax.rem(lax.div(me * rows, BLOCK), blocks_here)

    def finish(shard, turn):
        block = shard * blocks_here + lax.rem(my_place + 1 + turn, blocks_here)

        def mix(tile, inner):
            start = block * BLOCK + tile * QTILE
            here = pl.ds(pl.multiple_of(start, QTILE), QTILE)
            mixed = None
            for j in range(span):
                part = jnp.dot(
                    weights[here, j * BLOCK:(j + 1) * BLOCK], v_all[key_rows(block, j), :],
                    preferred_element_type=jnp.float32,
                )
                mixed = part if mixed is None else mixed + part
            o_all[here, :] = (mixed / total[here, :]).astype(jnp.bfloat16)

            def give(owner, carry):
                device = (block * tiles + tile) * owners + owner

                @pl.when(device != me)
                def _():
                    pltpu.make_async_remote_copy(
                        src_ref=o_all.at[rows_of(device), :],
                        dst_ref=out_ref.at[:, columns(me)],
                        send_sem=out_send_sem,
                        recv_sem=out_recv_sem,
                        device_id=(lax.div(device, group), lax.rem(device, group)),
                        device_id_type=MESH,
                    ).start()

                @pl.when(device == me)
                def _():
                    pltpu.make_async_copy(
                        o_all.at[rows_of(device), :], out_ref.at[:, columns(me)], out_own_sem
                    ).start()

                return carry

            return lax.fori_loop(0, owners, give, inner)

        lax.fori_loop(0, tiles, mix, 0)

    for back in range(3):
        arrived(2, back)

    def finish_previous(turn, carry):
        finish(lax.rem(my_blk + cycle - 1, cycle), turn)
        return carry

    lax.fori_loop(0, blocks_here, finish_previous, 0)
    for back in range(3, cycle):
        arrived(2, back)

    def finish_rest(step, carry):
        ahead = lax.rem(lax.rem(step, cycle - 1) + 1, cycle - 1)
        finish(lax.rem(my_blk + ahead, cycle), lax.div(step, cycle - 1))
        return carry

    lax.fori_loop(0, blocks_here * (cycle - 1), finish_rest, 0)

    pltpu.make_async_copy(
        o_all.at[rows_of(me), :], out_ref.at[:, columns(me)], out_own_sem
    ).wait()
    others = o_all.at[pl.ds(0, (count - 1) * rows), :]
    for index in range(3):
        pltpu.make_async_copy(others, others, send_sem.at[index]).wait()
    pltpu.make_async_copy(others, others, out_send_sem).wait()
    pltpu.make_async_copy(others, others, out_recv_sem).wait()


def local_heads(cycle, group, queries, keys, values, key_blocks, counts):
    rows, width = queries.shape
    tokens = rows * cycle * group
    blocks = tokens // BLOCK
    blocks_here = blocks // cycle
    span = 3 * blocks_here
    span = 3 * blocks_here
    whole = pltpu.VMEM((tokens, HD), jnp.bfloat16)
    return pl.pallas_call(
        functools.partial(head_kernel, cycle, group, blocks_here),
        out_shape=jax.ShapeDtypeStruct((rows, width), jnp.bfloat16),
        in_specs=[pl.BlockSpec(memory_space=pl.ANY)] * 5,
        out_specs=pl.BlockSpec(memory_space=pl.ANY),
        scratch_shapes=[
            whole, whole, whole, whole,
            pltpu.VMEM((span, QTILE, BLOCK), jnp.float32),
            pltpu.VMEM((tokens, span * BLOCK), jnp.bfloat16),
            pltpu.VMEM((tokens, 1), jnp.float32),
            pltpu.SMEM(key_blocks.shape, jnp.int32),
            pltpu.SMEM(counts.shape, jnp.int32),
            pltpu.SMEM((blocks, span), jnp.float32),
            pltpu.SemaphoreType.DMA((3,)),
            pltpu.SemaphoreType.DMA((3, cycle)),
            pltpu.SemaphoreType.DMA((3,)),
            pltpu.SemaphoreType.DMA((2,)),
            pltpu.SemaphoreType.DMA,
            pltpu.SemaphoreType.DMA,
            pltpu.SemaphoreType.DMA,
        ],
        compiler_params=pltpu.CompilerParams(
            collective_id=0, has_side_effects=True, vmem_limit_bytes=56 * 2**20
        ),
        cost_estimate=pl.CostEstimate(
            flops=4 * tokens * span * BLOCK * HD,
            bytes_accessed=8 * rows * width,
            transcendentals=tokens * span * BLOCK,
        ),
    )(queries, keys, values, key_blocks, counts)


def solution(mesh):
    cycle, group = mesh.shape["blk"], mesh.shape["head"]
    placed = (
        P(("blk", "head"), None),
        P(("blk", "head"), None),
        P(("blk", "head"), None),
        P(),
        P(),
    )
    one_head_each = cycle * group * HD

    def chosen(queries, *others):
        rows = queries.shape[0]
        aligned = QTILE % rows == 0 and rows * group % BLOCK == 0
        if queries.shape[1] == one_head_each and cycle >= 3 and group % 2 == 0 and aligned:
            return local_heads(cycle, group, queries, *others)
        return local(queries, *others)

    return jax.shard_map(
        chosen, mesh=mesh, in_specs=placed, out_specs=P(("blk", "head"), None), check_vma=False
    )
```

```python
import functools
import math

import jax
import jax.numpy as jnp
from jax import lax
from jax.experimental import pallas as pl
from jax.experimental.pallas import tpu as pltpu
from jax.sharding import PartitionSpec as P

HD = 128
BLOCK = 512
MAXB = 6


def from_behind(value, axis, steps):
    count = lax.axis_size(axis)
    pairs = [(source, (source + steps) % count) for source in range(count)]
    return lax.ppermute(value, axis, pairs)


def attend_shard(query_rows, context, listed_rows, count_rows):
    scale = HD ** (-0.5)
    group_rows = query_rows.shape[0]
    heads_local = query_rows.shape[1] // HD
    blocks_here = group_rows // BLOCK
    q_blocks = query_rows.reshape(blocks_here, BLOCK, heads_local, HD)
    pair_blocks = context.reshape(2, 3 * blocks_here, BLOCK, heads_local, HD)
    slot_ids = jnp.arange(MAXB, dtype=jnp.int32)

    def attend_block(inputs):
        query_block, listed, amount = inputs
        chosen = pair_blocks[:, listed]
        usable = (slot_ids < amount)[None, None, :, None]
        scores = (
            jnp.einsum("qhd,jkhd->hqjk", query_block, chosen[0], preferred_element_type=jnp.float32)
            * scale
        )
        top = jnp.max(jnp.where(usable, scores, -jnp.inf), axis=(2, 3), keepdims=True)
        expo = jnp.where(usable, jnp.exp(scores - top), 0.0)
        total = jnp.sum(expo, axis=(2, 3))
        weights = expo.astype(jnp.bfloat16)
        mixed = jnp.einsum("hqjk,jkhd->qhd", weights, chosen[1], preferred_element_type=jnp.float32)
        mixed = mixed / jnp.transpose(total)[:, :, None]
        return mixed.astype(jnp.bfloat16).reshape(BLOCK, heads_local * HD)

    result = lax.map(attend_block, (q_blocks, listed_rows, count_rows))
    return result.reshape(group_rows, heads_local * HD)


def local(queries, keys, values, key_blocks, counts):
    cycle_size = lax.axis_size("blk")
    query_rows = lax.all_to_all(queries, "head", split_axis=1, concat_axis=0, tiled=True)
    head_pair = lax.all_to_all(
        jnp.stack([keys, values]), "head", split_axis=2, concat_axis=1, tiled=True
    )
    earlier = from_behind(head_pair, "blk", 1)
    later = from_behind(head_pair, "blk", -1)
    context = jnp.concatenate([earlier, head_pair, later], axis=1)
    blocks_here = query_rows.shape[0] // BLOCK
    total_blocks = blocks_here * cycle_size
    first_block = lax.axis_index("blk") * blocks_here
    listed_rows = lax.dynamic_slice_in_dim(key_blocks, first_block, blocks_here, 0)
    count_rows = lax.dynamic_slice_in_dim(counts, first_block, blocks_here, 0)
    local_index = jnp.mod(listed_rows - first_block + blocks_here, total_blocks)
    attended_rows = attend_shard(query_rows, context, local_index, count_rows)
    return lax.all_to_all(attended_rows, "head", split_axis=0, concat_axis=1, tiled=True)


MESH = pl.DeviceIdType.MESH
QTILE = 256


def head_kernel(
    cycle, group, blocks_here, q_ref, k_ref, v_ref, lists_ref, counts_ref, out_ref,
    q_all, k_all, v_all, o_all, scores, weights, total, lists, amounts, bias_ref,
    send_sem, recv_sem, own_sem, list_sem, out_send_sem, out_recv_sem, out_own_sem,
):
    count = cycle * group
    rows = q_ref.shape[0]
    my_blk = lax.axis_index("blk")
    my_head = lax.axis_index("head")
    me = my_blk * group + my_head
    span = 3 * blocks_here
    blocks = cycle * blocks_here
    exponent = HD ** (-0.5) * math.log2(math.e)
    inputs = ((k_ref, k_all), (q_ref, q_all), (v_ref, v_all))

    def target(step):
        place = lax.rem(step, group)
        ahead = lax.div(place, 2) + (1 - lax.rem(place, 2)) * (group // 2)
        blk = lax.rem(my_blk + lax.div(step, group), cycle)
        head = lax.rem(my_head + ahead, group)
        return blk, head

    def columns(device):
        return pl.ds(pl.multiple_of(device * HD, HD), HD)

    def rows_of(device):
        return pl.ds(pl.multiple_of(device * rows, rows), rows)

    barrier = pltpu.get_barrier_semaphore()

    for step in range(count):
        if step != 1:
            pl.semaphore_signal(barrier, inc=1, device_id=target(step), device_id_type=MESH)
    pl.semaphore_wait(barrier, count - 1)

    def send_group(index, back):
        source, gathered = inputs[index]

        def send(step, carry):
            blk, head = target(step)
            pltpu.make_async_remote_copy(
                src_ref=source.at[:, columns(blk * group + head)],
                dst_ref=gathered.at[rows_of(me), :],
                send_sem=send_sem.at[index],
                recv_sem=recv_sem.at[index, back],
                device_id=(blk, head),
                device_id_type=MESH,
            ).start()
            return carry

        if back == 0:
            send(0, 0)
            lax.fori_loop(2, group, send, 0)
        else:
            lax.fori_loop(back * group, (back + 1) * group, send, 0)

    def own_copy(index):
        source, gathered = inputs[index]
        return pltpu.make_async_copy(
            source.at[:, columns(me)], gathered.at[rows_of(me), :], own_sem.at[index]
        )

    def arrived(index, back):
        gathered = inputs[index][1]
        if back == 0:
            own_copy(index).wait()
        senders = group - 1 if back == 0 else group
        part = gathered.at[pl.ds(0, senders * rows), :]
        pltpu.make_async_copy(part, part, recv_sem.at[index, back]).wait()

    def key_block(block, j):
        shard = lax.div(block, blocks_here)
        return lax.rem((shard + cycle - 1) * blocks_here + j, blocks)

    def key_rows(block, j):
        return pl.ds(pl.multiple_of(key_block(block, j) * BLOCK, BLOCK), BLOCK)

    later = (0,) + tuple(range(2, cycle))
    for back in range(3):
        send_group(0, back)
    send_group(1, 1)
    for back in range(3, cycle):
        send_group(0, back)
    for back in later:
        send_group(1, back)
    for index in range(3):
        own_copy(index).start()
    list_copies = (
        pltpu.make_async_copy(lists_ref, lists, list_sem.at[0]),
        pltpu.make_async_copy(counts_ref, amounts, list_sem.at[1]),
    )
    for copy in list_copies:
        copy.start()
    for copy in list_copies:
        copy.wait()

    def mark(block, carry):
        for j in range(span):
            offered = key_block(block, j)
            hits = jnp.int32(0)
            for slot in range(MAXB):
                same = lists[block, slot] == offered
                hits += jnp.where(same & (slot < amounts[block]), 1, 0)
            bias_ref[block, j] = jnp.where(hits > 0, 0.0, -jnp.inf)
        return carry

    lax.fori_loop(0, blocks, mark, 0)

    for back in range(3):
        arrived(0, back)
    for back in range(cycle):
        send_group(2, back)
    tiles = BLOCK // QTILE

    def weigh(step, carry):
        block = lax.div(step, tiles)
        here = pl.ds(pl.multiple_of(step * QTILE, QTILE), QTILE)
        query = q_all[here, :]
        top = None
        for j in range(span):
            part = lax.dot_general(
                query, k_all[key_rows(block, j), :], (((1,), (1,)), ((), ())),
                preferred_element_type=jnp.float32,
            )
            scores[j] = part
            part_top = jnp.max(part, axis=1, keepdims=True) + bias_ref[block, j]
            top = part_top if top is None else jnp.maximum(top, part_top)
        shift = top * exponent
        amount = None
        for j in range(span):
            expo = jnp.exp2(scores[j] * exponent + (bias_ref[block, j] - shift))
            weights[here, j * BLOCK:(j + 1) * BLOCK] = expo.astype(jnp.bfloat16)
            part_sum = jnp.sum(expo, axis=1, keepdims=True)
            amount = part_sum if amount is None else amount + part_sum
        total[here, :] = amount
        return carry

    per_shard = blocks_here * tiles
    def weigh_shard(back):
        arrived(1, back)
        first = lax.rem(my_blk + cycle - back, cycle) * per_shard

        def weigh_here(step, carry):
            return weigh(first + step, carry)

        lax.fori_loop(0, per_shard, weigh_here, 0)

    weigh_shard(1)
    for back in range(3, cycle):
        arrived(0, back)
    for back in later:
        weigh_shard(back)

    owners = QTILE // rows
    my_place = lax.rem(lax.div(me * rows, BLOCK), blocks_here)

    def finish(shard):
        def mix(step, inner):
            turn, tile = lax.rem(step, blocks_here), lax.div(step, blocks_here)
            block = shard * blocks_here + lax.rem(my_place + 1 + turn, blocks_here)
            start = block * BLOCK + tile * QTILE
            here = pl.ds(pl.multiple_of(start, QTILE), QTILE)
            mixed = None
            for j in range(span):
                part = jnp.dot(
                    weights[here, j * BLOCK:(j + 1) * BLOCK], v_all[key_rows(block, j), :],
                    preferred_element_type=jnp.float32,
                )
                mixed = part if mixed is None else mixed + part
            o_all[here, :] = (mixed / total[here, :]).astype(jnp.bfloat16)

            def give(owner, carry):
                device = (block * tiles + tile) * owners + owner

                @pl.when(device != me)
                def _():
                    pltpu.make_async_remote_copy(
                        src_ref=o_all.at[rows_of(device), :],
                        dst_ref=out_ref.at[:, columns(me)],
                        send_sem=out_send_sem,
                        recv_sem=out_recv_sem,
                        device_id=(lax.div(device, group), lax.rem(device, group)),
                        device_id_type=MESH,
                    ).start()

                @pl.when(device == me)
                def _():
                    pltpu.make_async_copy(
                        o_all.at[rows_of(device), :], out_ref.at[:, columns(me)], out_own_sem
                    ).start()

                return carry

            return lax.fori_loop(0, owners, give, inner)

        lax.fori_loop(0, blocks_here * tiles, mix, 0)

    for back in range(3):
        arrived(2, back)

    finish(lax.rem(my_blk + cycle - 1, cycle))
    for back in range(3, cycle):
        arrived(2, back)

    def finish_rest(step, carry):
        ahead = lax.rem(step + 1, cycle - 1)
        finish(lax.rem(my_blk + ahead, cycle))
        return carry

    lax.fori_loop(0, cycle - 1, finish_rest, 0)

    pltpu.make_async_copy(
        o_all.at[rows_of(me), :], out_ref.at[:, columns(me)], out_own_sem
    ).wait()
    others = o_all.at[pl.ds(0, (count - 1) * rows), :]
    for index in range(3):
        pltpu.make_async_copy(others, others, send_sem.at[index]).wait()
    pltpu.make_async_copy(others, others, out_send_sem).wait()
    pltpu.make_async_copy(others, others, out_recv_sem).wait()


def rows_kernel(pieces, source, result, sems):
    rows = source.shape[0] // pieces
    copies = []
    for piece in range(pieces):
        here = pl.ds(piece * rows, rows)
        copies.append(pltpu.make_async_copy(source.at[here], result.at[here], sems.at[piece]))
    for copy in copies:
        copy.start()
    for copy in copies:
        copy.wait()


def place_rows(array):
    pieces = array.shape[0] // 16
    return pl.pallas_call(
        functools.partial(rows_kernel, pieces),
        out_shape=jax.ShapeDtypeStruct(array.shape, array.dtype),
        in_specs=[pl.BlockSpec(memory_space=pl.ANY)],
        out_specs=pl.BlockSpec(memory_space=pl.ANY),
        scratch_shapes=[pltpu.SemaphoreType.DMA((pieces,))],
        compiler_params=pltpu.CompilerParams(vmem_limit_bytes=60 * 2**20),
    )(array)


def local_heads(cycle, group, queries, keys, values, key_blocks, counts):
    rows, width = queries.shape
    tokens = rows * cycle * group
    blocks = tokens // BLOCK
    blocks_here = blocks // cycle
    span = 3 * blocks_here
    span = 3 * blocks_here
    whole = pltpu.VMEM((tokens, HD), jnp.bfloat16)
    attended = pl.pallas_call(
        functools.partial(head_kernel, cycle, group, blocks_here),
        out_shape=jax.ShapeDtypeStruct((rows, width), jnp.bfloat16),
        in_specs=[pl.BlockSpec(memory_space=pl.ANY)] * 5,
        out_specs=pl.BlockSpec(memory_space=pl.ANY),
        scratch_shapes=[
            whole, whole, whole, whole,
            pltpu.VMEM((span, QTILE, BLOCK), jnp.float32),
            pltpu.VMEM((tokens, span * BLOCK), jnp.bfloat16),
            pltpu.VMEM((tokens, 1), jnp.float32),
            pltpu.SMEM(key_blocks.shape, jnp.int32),
            pltpu.SMEM(counts.shape, jnp.int32),
            pltpu.SMEM((blocks, span), jnp.float32),
            pltpu.SemaphoreType.DMA((3,)),
            pltpu.SemaphoreType.DMA((3, cycle)),
            pltpu.SemaphoreType.DMA((3,)),
            pltpu.SemaphoreType.DMA((2,)),
            pltpu.SemaphoreType.DMA,
            pltpu.SemaphoreType.DMA,
            pltpu.SemaphoreType.DMA,
        ],
        compiler_params=pltpu.CompilerParams(
            collective_id=0, has_side_effects=True, vmem_limit_bytes=56 * 2**20
        ),
        cost_estimate=pl.CostEstimate(
            flops=4 * tokens * span * BLOCK * HD,
            bytes_accessed=8 * rows * width,
            transcendentals=tokens * span * BLOCK,
        ),
    )(queries, keys, values, key_blocks, counts)
    return place_rows(attended)


def solution(mesh):
    cycle, group = mesh.shape["blk"], mesh.shape["head"]
    placed = (
        P(("blk", "head"), None),
        P(("blk", "head"), None),
        P(("blk", "head"), None),
        P(),
        P(),
    )
    one_head_each = cycle * group * HD

    def chosen(queries, *others):
        rows = queries.shape[0]
        aligned = QTILE % rows == 0 and rows % 16 == 0 and rows * group % BLOCK == 0
        if queries.shape[1] == one_head_each and cycle >= 3 and group % 2 == 0 and aligned:
            return local_heads(cycle, group, queries, *others)
        return local(queries, *others)

    return jax.shard_map(
        chosen, mesh=mesh, in_specs=placed, out_specs=P(("blk", "head"), None), check_vma=False
    )
```

```python
import functools
import math

import jax
import jax.numpy as jnp
from jax import lax
from jax.experimental import pallas as pl
from jax.experimental.pallas import tpu as pltpu
from jax.sharding import PartitionSpec as P

HD = 128
BLOCK = 512
MAXB = 6


def from_behind(value, axis, steps):
    count = lax.axis_size(axis)
    pairs = [(source, (source + steps) % count) for source in range(count)]
    return lax.ppermute(value, axis, pairs)


def attend_shard(query_rows, context, listed_rows, count_rows):
    scale = HD ** (-0.5)
    group_rows = query_rows.shape[0]
    heads_local = query_rows.shape[1] // HD
    blocks_here = group_rows // BLOCK
    q_blocks = query_rows.reshape(blocks_here, BLOCK, heads_local, HD)
    pair_blocks = context.reshape(2, 3 * blocks_here, BLOCK, heads_local, HD)
    slot_ids = jnp.arange(MAXB, dtype=jnp.int32)

    def attend_block(inputs):
        query_block, listed, amount = inputs
        chosen = pair_blocks[:, listed]
        usable = (slot_ids < amount)[None, None, :, None]
        scores = (
            jnp.einsum("qhd,jkhd->hqjk", query_block, chosen[0], preferred_element_type=jnp.float32)
            * scale
        )
        top = jnp.max(jnp.where(usable, scores, -jnp.inf), axis=(2, 3), keepdims=True)
        expo = jnp.where(usable, jnp.exp(scores - top), 0.0)
        total = jnp.sum(expo, axis=(2, 3))
        weights = expo.astype(jnp.bfloat16)
        mixed = jnp.einsum("hqjk,jkhd->qhd", weights, chosen[1], preferred_element_type=jnp.float32)
        mixed = mixed / jnp.transpose(total)[:, :, None]
        return mixed.astype(jnp.bfloat16).reshape(BLOCK, heads_local * HD)

    result = lax.map(attend_block, (q_blocks, listed_rows, count_rows))
    return result.reshape(group_rows, heads_local * HD)


def local(queries, keys, values, key_blocks, counts):
    cycle_size = lax.axis_size("blk")
    query_rows = lax.all_to_all(queries, "head", split_axis=1, concat_axis=0, tiled=True)
    head_pair = lax.all_to_all(
        jnp.stack([keys, values]), "head", split_axis=2, concat_axis=1, tiled=True
    )
    earlier = from_behind(head_pair, "blk", 1)
    later = from_behind(head_pair, "blk", -1)
    context = jnp.concatenate([earlier, head_pair, later], axis=1)
    blocks_here = query_rows.shape[0] // BLOCK
    total_blocks = blocks_here * cycle_size
    first_block = lax.axis_index("blk") * blocks_here
    listed_rows = lax.dynamic_slice_in_dim(key_blocks, first_block, blocks_here, 0)
    count_rows = lax.dynamic_slice_in_dim(counts, first_block, blocks_here, 0)
    local_index = jnp.mod(listed_rows - first_block + blocks_here, total_blocks)
    attended_rows = attend_shard(query_rows, context, local_index, count_rows)
    return lax.all_to_all(attended_rows, "head", split_axis=0, concat_axis=1, tiled=True)


MESH = pl.DeviceIdType.MESH
QTILE = 256


def head_kernel(
    cycle, group, blocks_here, q_ref, k_ref, v_ref, lists_ref, counts_ref, out_ref,
    q_all, k_all, v_all, o_all, scores, weights, total, lists, amounts, bias_ref,
    send_sem, recv_sem, own_sem, list_sem, out_send_sem, out_recv_sem, out_own_sem,
):
    count = cycle * group
    rows = q_ref.shape[0]
    my_blk = lax.axis_index("blk")
    my_head = lax.axis_index("head")
    me = my_blk * group + my_head
    span = 3 * blocks_here
    blocks = cycle * blocks_here
    exponent = HD ** (-0.5) * math.log2(math.e)
    inputs = ((k_ref, k_all), (q_ref, q_all), (v_ref, v_all))

    def target(step):
        place = lax.rem(step, group)
        ahead = lax.div(place, 2) + (1 - lax.rem(place, 2)) * (group // 2)
        blk = lax.rem(my_blk + lax.div(step, group), cycle)
        head = lax.rem(my_head + ahead, group)
        return blk, head

    def columns(device):
        return pl.ds(pl.multiple_of(device * HD, HD), HD)

    def rows_of(device):
        return pl.ds(pl.multiple_of(device * rows, rows), rows)

    barrier = pltpu.get_barrier_semaphore()

    for step in range(count):
        if step != 1:
            pl.semaphore_signal(barrier, inc=1, device_id=target(step), device_id_type=MESH)
    pl.semaphore_wait(barrier, count - 1)

    def send_group(index, back):
        source, gathered = inputs[index]

        def send(step, carry):
            blk, head = target(step)
            pltpu.make_async_remote_copy(
                src_ref=source.at[:, columns(blk * group + head)],
                dst_ref=gathered.at[rows_of(me), :],
                send_sem=send_sem.at[index],
                recv_sem=recv_sem.at[index, back],
                device_id=(blk, head),
                device_id_type=MESH,
            ).start()
            return carry

        if back == 0:
            send(0, 0)
            lax.fori_loop(2, group, send, 0)
        else:
            lax.fori_loop(back * group, (back + 1) * group, send, 0)

    def own_copy(index):
        source, gathered = inputs[index]
        return pltpu.make_async_copy(
            source.at[:, columns(me)], gathered.at[rows_of(me), :], own_sem.at[index]
        )

    def arrived(index, back):
        gathered = inputs[index][1]
        if back == 0:
            own_copy(index).wait()
        senders = group - 1 if back == 0 else group
        part = gathered.at[pl.ds(0, senders * rows), :]
        pltpu.make_async_copy(part, part, recv_sem.at[index, back]).wait()

    def key_block(block, j):
        shard = lax.div(block, blocks_here)
        return lax.rem((shard + cycle - 1) * blocks_here + j, blocks)

    def key_rows(block, j):
        return pl.ds(pl.multiple_of(key_block(block, j) * BLOCK, BLOCK), BLOCK)

    later = (0,) + tuple(range(2, cycle))
    for back in range(3):
        send_group(0, back)
    send_group(1, 1)
    for back in range(3, cycle):
        send_group(0, back)
    for back in later:
        send_group(1, back)
    for index in range(3):
        own_copy(index).start()
    list_copies = (
        pltpu.make_async_copy(lists_ref, lists, list_sem.at[0]),
        pltpu.make_async_copy(counts_ref, amounts, list_sem.at[1]),
    )
    for copy in list_copies:
        copy.start()
    for copy in list_copies:
        copy.wait()

    def mark(block, carry):
        for j in range(span):
            offered = key_block(block, j)
            hits = jnp.int32(0)
            for slot in range(MAXB):
                same = lists[block, slot] == offered
                hits += jnp.where(same & (slot < amounts[block]), 1, 0)
            bias_ref[block, j] = jnp.where(hits > 0, 0.0, -jnp.inf)
        return carry

    lax.fori_loop(0, blocks, mark, 0)

    for back in range(3):
        arrived(0, back)
    for back in range(cycle):
        send_group(2, back)
    tiles = BLOCK // QTILE

    def weigh(step, carry):
        block = lax.div(step, tiles)
        here = pl.ds(pl.multiple_of(step * QTILE, QTILE), QTILE)
        query = q_all[here, :]
        top = None
        for j in range(span):
            part = lax.dot_general(
                query, k_all[key_rows(block, j), :], (((1,), (1,)), ((), ())),
                preferred_element_type=jnp.float32,
            )
            scores[j] = part
            part_top = jnp.max(part, axis=1, keepdims=True) + bias_ref[block, j]
            top = part_top if top is None else jnp.maximum(top, part_top)
        shift = top * exponent
        amount = None
        for j in range(span):
            expo = jnp.exp2(scores[j] * exponent + (bias_ref[block, j] - shift))
            weights[here, j * BLOCK:(j + 1) * BLOCK] = expo.astype(jnp.bfloat16)
            part_sum = jnp.sum(expo, axis=1, keepdims=True)
            amount = part_sum if amount is None else amount + part_sum
        total[here, :] = amount
        return carry

    per_shard = blocks_here * tiles
    def weigh_shard(back):
        arrived(1, back)
        first = lax.rem(my_blk + cycle - back, cycle) * per_shard

        def weigh_here(step, carry):
            return weigh(first + step, carry)

        lax.fori_loop(0, per_shard, weigh_here, 0)

    weigh_shard(1)
    for back in range(3, cycle):
        arrived(0, back)
    for back in later:
        weigh_shard(back)

    owners = QTILE // rows
    my_place = lax.rem(lax.div(me * rows, BLOCK), blocks_here)

    def finish(shard):
        def mix(step, inner):
            turn, tile = lax.rem(step, blocks_here), lax.div(step, blocks_here)
            block = shard * blocks_here + lax.rem(my_place + 1 + turn, blocks_here)
            start = block * BLOCK + tile * QTILE
            here = pl.ds(pl.multiple_of(start, QTILE), QTILE)
            mixed = None
            for j in range(span):
                part = jnp.dot(
                    weights[here, j * BLOCK:(j + 1) * BLOCK], v_all[key_rows(block, j), :],
                    preferred_element_type=jnp.float32,
                )
                mixed = part if mixed is None else mixed + part
            o_all[here, :] = (mixed / total[here, :]).astype(jnp.bfloat16)

            def give(owner, carry):
                device = (block * tiles + tile) * owners + owner

                @pl.when(device != me)
                def _():
                    pltpu.make_async_remote_copy(
                        src_ref=o_all.at[rows_of(device), :],
                        dst_ref=out_ref.at[:, columns(me)],
                        send_sem=out_send_sem,
                        recv_sem=out_recv_sem,
                        device_id=(lax.div(device, group), lax.rem(device, group)),
                        device_id_type=MESH,
                    ).start()

                @pl.when(device == me)
                def _():
                    pltpu.make_async_copy(
                        o_all.at[rows_of(device), :], out_ref.at[:, columns(me)], out_own_sem
                    ).start()

                return carry

            return lax.fori_loop(0, owners, give, inner)

        lax.fori_loop(0, blocks_here * tiles, mix, 0)

    for back in range(3):
        arrived(2, back)

    finish(lax.rem(my_blk + cycle - 1, cycle))
    for back in range(3, cycle):
        arrived(2, back)

    def finish_rest(step, carry):
        ahead = lax.rem(step + 1, cycle - 1)
        finish(lax.rem(my_blk + ahead, cycle))
        return carry

    lax.fori_loop(0, cycle - 1, finish_rest, 0)

    pltpu.make_async_copy(
        o_all.at[rows_of(me), :], out_ref.at[:, columns(me)], out_own_sem
    ).wait()
    others = o_all.at[pl.ds(0, (count - 1) * rows), :]
    for index in range(3):
        pltpu.make_async_copy(others, others, send_sem.at[index]).wait()
    pltpu.make_async_copy(others, others, out_send_sem).wait()
    pltpu.make_async_copy(others, others, out_recv_sem).wait()


def rows_kernel(source, result):
    result[...] = source[...]


def place_rows(array):
    rows, width = array.shape
    piece = pl.BlockSpec((rows // 4, width), lambda step: (step, 0))
    return pl.pallas_call(
        rows_kernel,
        grid=(4,),
        out_shape=jax.ShapeDtypeStruct(array.shape, array.dtype),
        in_specs=[piece],
        out_specs=piece,
        compiler_params=pltpu.CompilerParams(vmem_limit_bytes=60 * 2**20),
    )(array)


def local_heads(cycle, group, queries, keys, values, key_blocks, counts):
    rows, width = queries.shape
    tokens = rows * cycle * group
    blocks = tokens // BLOCK
    blocks_here = blocks // cycle
    span = 3 * blocks_here
    span = 3 * blocks_here
    whole = pltpu.VMEM((tokens, HD), jnp.bfloat16)
    attended = pl.pallas_call(
        functools.partial(head_kernel, cycle, group, blocks_here),
        out_shape=jax.ShapeDtypeStruct((rows, width), jnp.bfloat16),
        in_specs=[pl.BlockSpec(memory_space=pl.ANY)] * 5,
        out_specs=pl.BlockSpec(memory_space=pl.ANY),
        scratch_shapes=[
            whole, whole, whole, whole,
            pltpu.VMEM((span, QTILE, BLOCK), jnp.float32),
            pltpu.VMEM((tokens, span * BLOCK), jnp.bfloat16),
            pltpu.VMEM((tokens, 1), jnp.float32),
            pltpu.SMEM(key_blocks.shape, jnp.int32),
            pltpu.SMEM(counts.shape, jnp.int32),
            pltpu.SMEM((blocks, span), jnp.float32),
            pltpu.SemaphoreType.DMA((3,)),
            pltpu.SemaphoreType.DMA((3, cycle)),
            pltpu.SemaphoreType.DMA((3,)),
            pltpu.SemaphoreType.DMA((2,)),
            pltpu.SemaphoreType.DMA,
            pltpu.SemaphoreType.DMA,
            pltpu.SemaphoreType.DMA,
        ],
        compiler_params=pltpu.CompilerParams(
            collective_id=0, has_side_effects=True, vmem_limit_bytes=56 * 2**20
        ),
        cost_estimate=pl.CostEstimate(
            flops=4 * tokens * span * BLOCK * HD,
            bytes_accessed=8 * rows * width,
            transcendentals=tokens * span * BLOCK,
        ),
    )(queries, keys, values, key_blocks, counts)
    return place_rows(attended)


def solution(mesh):
    cycle, group = mesh.shape["blk"], mesh.shape["head"]
    placed = (
        P(("blk", "head"), None),
        P(("blk", "head"), None),
        P(("blk", "head"), None),
        P(),
        P(),
    )
    one_head_each = cycle * group * HD

    def chosen(queries, *others):
        rows = queries.shape[0]
        aligned = QTILE % rows == 0 and rows % 64 == 0 and rows * group % BLOCK == 0
        if queries.shape[1] == one_head_each and cycle >= 3 and group % 2 == 0 and aligned:
            return local_heads(cycle, group, queries, *others)
        return local(queries, *others)

    return jax.shard_map(
        chosen, mesh=mesh, in_specs=placed, out_specs=P(("blk", "head"), None), check_vma=False
    )
```

```python
import functools
import math

import jax
import jax.numpy as jnp
from jax import lax
from jax.experimental import pallas as pl
from jax.experimental.pallas import tpu as pltpu
from jax.sharding import PartitionSpec as P

HD = 128
BLOCK = 512
MAXB = 6


def from_behind(value, axis, steps):
    count = lax.axis_size(axis)
    pairs = [(source, (source + steps) % count) for source in range(count)]
    return lax.ppermute(value, axis, pairs)


def attend_shard(query_rows, context, listed_rows, count_rows):
    scale = HD ** (-0.5)
    group_rows = query_rows.shape[0]
    heads_local = query_rows.shape[1] // HD
    blocks_here = group_rows // BLOCK
    q_blocks = query_rows.reshape(blocks_here, BLOCK, heads_local, HD)
    pair_blocks = context.reshape(2, 3 * blocks_here, BLOCK, heads_local, HD)
    slot_ids = jnp.arange(MAXB, dtype=jnp.int32)

    def attend_block(inputs):
        query_block, listed, amount = inputs
        chosen = pair_blocks[:, listed]
        usable = (slot_ids < amount)[None, None, :, None]
        scores = (
            jnp.einsum("qhd,jkhd->hqjk", query_block, chosen[0], preferred_element_type=jnp.float32)
            * scale
        )
        top = jnp.max(jnp.where(usable, scores, -jnp.inf), axis=(2, 3), keepdims=True)
        expo = jnp.where(usable, jnp.exp(scores - top), 0.0)
        total = jnp.sum(expo, axis=(2, 3))
        weights = expo.astype(jnp.bfloat16)
        mixed = jnp.einsum("hqjk,jkhd->qhd", weights, chosen[1], preferred_element_type=jnp.float32)
        mixed = mixed / jnp.transpose(total)[:, :, None]
        return mixed.astype(jnp.bfloat16).reshape(BLOCK, heads_local * HD)

    result = lax.map(attend_block, (q_blocks, listed_rows, count_rows))
    return result.reshape(group_rows, heads_local * HD)


def local(queries, keys, values, key_blocks, counts):
    cycle_size = lax.axis_size("blk")
    query_rows = lax.all_to_all(queries, "head", split_axis=1, concat_axis=0, tiled=True)
    head_pair = lax.all_to_all(
        jnp.stack([keys, values]), "head", split_axis=2, concat_axis=1, tiled=True
    )
    earlier = from_behind(head_pair, "blk", 1)
    later = from_behind(head_pair, "blk", -1)
    context = jnp.concatenate([earlier, head_pair, later], axis=1)
    blocks_here = query_rows.shape[0] // BLOCK
    total_blocks = blocks_here * cycle_size
    first_block = lax.axis_index("blk") * blocks_here
    listed_rows = lax.dynamic_slice_in_dim(key_blocks, first_block, blocks_here, 0)
    count_rows = lax.dynamic_slice_in_dim(counts, first_block, blocks_here, 0)
    local_index = jnp.mod(listed_rows - first_block + blocks_here, total_blocks)
    attended_rows = attend_shard(query_rows, context, local_index, count_rows)
    return lax.all_to_all(attended_rows, "head", split_axis=0, concat_axis=1, tiled=True)


MESH = pl.DeviceIdType.MESH
QTILE = 256


def head_kernel(
    cycle, group, blocks_here, q_ref, k_ref, v_ref, lists_ref, counts_ref, out_ref,
    q_all, k_all, v_all, o_all, scores, weights, total, lists, amounts, bias_ref,
    send_sem, recv_sem, own_sem, list_sem, out_send_sem, out_recv_sem, out_own_sem,
):
    count = cycle * group
    rows = q_ref.shape[0]
    my_blk = lax.axis_index("blk")
    my_head = lax.axis_index("head")
    me = my_blk * group + my_head
    span = 3 * blocks_here
    blocks = cycle * blocks_here
    exponent = HD ** (-0.5) * math.log2(math.e)
    inputs = ((k_ref, k_all), (q_ref, q_all), (v_ref, v_all))

    def target(step):
        place = lax.rem(step, group)
        ahead = lax.div(place, 2) + (1 - lax.rem(place, 2)) * (group // 2)
        blk = lax.rem(my_blk + lax.div(step, group), cycle)
        head = lax.rem(my_head + ahead, group)
        return blk, head

    def columns(device):
        return pl.ds(pl.multiple_of(device * HD, HD), HD)

    def rows_of(device):
        return pl.ds(pl.multiple_of(device * rows, rows), rows)

    barrier = pltpu.get_barrier_semaphore()

    for step in range(count):
        if step != 1:
            pl.semaphore_signal(barrier, inc=1, device_id=target(step), device_id_type=MESH)
    pl.semaphore_wait(barrier, count - 1)

    def send_group(index, back):
        source, gathered = inputs[index]

        def send(step, carry):
            blk, head = target(step)
            pltpu.make_async_remote_copy(
                src_ref=source.at[:, columns(blk * group + head)],
                dst_ref=gathered.at[rows_of(me), :],
                send_sem=send_sem.at[index],
                recv_sem=recv_sem.at[index, back],
                device_id=(blk, head),
                device_id_type=MESH,
            ).start()
            return carry

        if back == 0:
            send(0, 0)
            lax.fori_loop(2, group, send, 0, unroll=True)
        else:
            lax.fori_loop(back * group, (back + 1) * group, send, 0, unroll=True)

    def own_copy(index):
        source, gathered = inputs[index]
        return pltpu.make_async_copy(
            source.at[:, columns(me)], gathered.at[rows_of(me), :], own_sem.at[index]
        )

    def arrived(index, back):
        gathered = inputs[index][1]
        if back == 0:
            own_copy(index).wait()
        senders = group - 1 if back == 0 else group
        part = gathered.at[pl.ds(0, senders * rows), :]
        pltpu.make_async_copy(part, part, recv_sem.at[index, back]).wait()

    def key_block(block, j):
        shard = lax.div(block, blocks_here)
        return lax.rem((shard + cycle - 1) * blocks_here + j, blocks)

    def key_rows(block, j):
        return pl.ds(pl.multiple_of(key_block(block, j) * BLOCK, BLOCK), BLOCK)

    later = (0,) + tuple(range(2, cycle))
    for back in range(3):
        send_group(0, back)
    send_group(1, 1)
    for back in range(3, cycle):
        send_group(0, back)
    for back in later:
        send_group(1, back)
    for index in range(3):
        own_copy(index).start()
    list_copies = (
        pltpu.make_async_copy(lists_ref, lists, list_sem.at[0]),
        pltpu.make_async_copy(counts_ref, amounts, list_sem.at[1]),
    )
    for copy in list_copies:
        copy.start()
    for copy in list_copies:
        copy.wait()

    def mark(block, carry):
        for j in range(span):
            offered = key_block(block, j)
            hits = jnp.int32(0)
            for slot in range(MAXB):
                same = lists[block, slot] == offered
                hits += jnp.where(same & (slot < amounts[block]), 1, 0)
            bias_ref[block, j] = jnp.where(hits > 0, 0.0, -jnp.inf)
        return carry

    lax.fori_loop(0, blocks, mark, 0)

    for back in range(3):
        arrived(0, back)
    for back in range(cycle):
        send_group(2, back)
    tiles = BLOCK // QTILE

    def weigh(step, carry):
        block = lax.div(step, tiles)
        here = pl.ds(pl.multiple_of(step * QTILE, QTILE), QTILE)
        query = q_all[here, :]
        top = None
        for j in range(span):
            part = lax.dot_general(
                query, k_all[key_rows(block, j), :], (((1,), (1,)), ((), ())),
                preferred_element_type=jnp.float32,
            )
            scores[j] = part
            part_top = jnp.max(part, axis=1, keepdims=True) + bias_ref[block, j]
            top = part_top if top is None else jnp.maximum(top, part_top)
        shift = top * exponent
        amount = None
        for j in range(span):
            expo = jnp.exp2(scores[j] * exponent + (bias_ref[block, j] - shift))
            weights[here, j * BLOCK:(j + 1) * BLOCK] = expo.astype(jnp.bfloat16)
            part_sum = jnp.sum(expo, axis=1, keepdims=True)
            amount = part_sum if amount is None else amount + part_sum
        total[here, :] = amount
        return carry

    per_shard = blocks_here * tiles
    def weigh_shard(back):
        arrived(1, back)
        first = lax.rem(my_blk + cycle - back, cycle) * per_shard

        def weigh_here(step, carry):
            return weigh(first + step, carry)

        lax.fori_loop(0, per_shard, weigh_here, 0)

    weigh_shard(1)
    for back in range(3, cycle):
        arrived(0, back)
    for back in later:
        weigh_shard(back)

    owners = QTILE // rows
    my_place = lax.rem(lax.div(me * rows, BLOCK), blocks_here)

    def finish(shard, turn):
        block = shard * blocks_here + lax.rem(my_place + 1 + turn, blocks_here)

        def mix(tile, inner):
            start = block * BLOCK + tile * QTILE
            here = pl.ds(pl.multiple_of(start, QTILE), QTILE)
            mixed = None
            for j in range(span):
                part = jnp.dot(
                    weights[here, j * BLOCK:(j + 1) * BLOCK], v_all[key_rows(block, j), :],
                    preferred_element_type=jnp.float32,
                )
                mixed = part if mixed is None else mixed + part
            o_all[here, :] = (mixed / total[here, :]).astype(jnp.bfloat16)

            def give(owner, carry):
                device = (block * tiles + tile) * owners + owner

                @pl.when(device != me)
                def _():
                    pltpu.make_async_remote_copy(
                        src_ref=o_all.at[rows_of(device), :],
                        dst_ref=out_ref.at[:, columns(me)],
                        send_sem=out_send_sem,
                        recv_sem=out_recv_sem,
                        device_id=(lax.div(device, group), lax.rem(device, group)),
                        device_id_type=MESH,
                    ).start()

                @pl.when(device == me)
                def _():
                    pltpu.make_async_copy(
                        o_all.at[rows_of(device), :], out_ref.at[:, columns(me)], out_own_sem
                    ).start()

                return carry

            return lax.fori_loop(0, owners, give, inner)

        lax.fori_loop(0, tiles, mix, 0)

    for back in range(3):
        arrived(2, back)

    def finish_previous(turn, carry):
        finish(lax.rem(my_blk + cycle - 1, cycle), turn)
        return carry

    lax.fori_loop(0, blocks_here, finish_previous, 0)
    for back in range(3, cycle):
        arrived(2, back)

    def finish_rest(step, carry):
        ahead = lax.rem(lax.rem(step, cycle - 1) + 1, cycle - 1)
        finish(lax.rem(my_blk + ahead, cycle), lax.div(step, cycle - 1))
        return carry

    lax.fori_loop(0, blocks_here * (cycle - 1), finish_rest, 0)

    pltpu.make_async_copy(
        o_all.at[rows_of(me), :], out_ref.at[:, columns(me)], out_own_sem
    ).wait()
    others = o_all.at[pl.ds(0, (count - 1) * rows), :]
    for index in range(3):
        pltpu.make_async_copy(others, others, send_sem.at[index]).wait()
    pltpu.make_async_copy(others, others, out_send_sem).wait()
    pltpu.make_async_copy(others, others, out_recv_sem).wait()


def local_heads(cycle, group, queries, keys, values, key_blocks, counts):
    rows, width = queries.shape
    tokens = rows * cycle * group
    blocks = tokens // BLOCK
    blocks_here = blocks // cycle
    span = 3 * blocks_here
    span = 3 * blocks_here
    whole = pltpu.VMEM((tokens, HD), jnp.bfloat16)
    return pl.pallas_call(
        functools.partial(head_kernel, cycle, group, blocks_here),
        out_shape=jax.ShapeDtypeStruct((rows, width), jnp.bfloat16),
        in_specs=[pl.BlockSpec(memory_space=pl.ANY)] * 5,
        out_specs=pl.BlockSpec(memory_space=pl.ANY),
        scratch_shapes=[
            whole, whole, whole, whole,
            pltpu.VMEM((span, QTILE, BLOCK), jnp.float32),
            pltpu.VMEM((tokens, span * BLOCK), jnp.bfloat16),
            pltpu.VMEM((tokens, 1), jnp.float32),
            pltpu.SMEM(key_blocks.shape, jnp.int32),
            pltpu.SMEM(counts.shape, jnp.int32),
            pltpu.SMEM((blocks, span), jnp.float32),
            pltpu.SemaphoreType.DMA((3,)),
            pltpu.SemaphoreType.DMA((3, cycle)),
            pltpu.SemaphoreType.DMA((3,)),
            pltpu.SemaphoreType.DMA((2,)),
            pltpu.SemaphoreType.DMA,
            pltpu.SemaphoreType.DMA,
            pltpu.SemaphoreType.DMA,
        ],
        compiler_params=pltpu.CompilerParams(
            collective_id=0, has_side_effects=True, vmem_limit_bytes=56 * 2**20
        ),
        cost_estimate=pl.CostEstimate(
            flops=4 * tokens * span * BLOCK * HD,
            bytes_accessed=8 * rows * width,
            transcendentals=tokens * span * BLOCK,
        ),
    )(queries, keys, values, key_blocks, counts)


def solution(mesh):
    cycle, group = mesh.shape["blk"], mesh.shape["head"]
    placed = (
        P(("blk", "head"), None),
        P(("blk", "head"), None),
        P(("blk", "head"), None),
        P(),
        P(),
    )
    one_head_each = cycle * group * HD

    def chosen(queries, *others):
        rows = queries.shape[0]
        aligned = QTILE % rows == 0 and rows * group % BLOCK == 0
        if queries.shape[1] == one_head_each and cycle >= 3 and group % 2 == 0 and aligned:
            return local_heads(cycle, group, queries, *others)
        return local(queries, *others)

    return jax.shard_map(
        chosen, mesh=mesh, in_specs=placed, out_specs=P(("blk", "head"), None), check_vma=False
    )
```
